256 devices in a mesh: dp: 32 (over y, x, core), seq: 8 (over z).
Axes of the slice: x: 4, y: 4, z: 8, core: 2. Of those that a mesh axis runs over, the one named last changes fastest.
Arguments:
- clip_table: int32 [64, 5], replicated, may hold values from 0 to 31, as said below
- attention_inputs: bfloat16 [3, 32768, 3072], P(None, ('dp', 'seq')), may hold values from -24 to 24
- out_weight: bfloat16 [3072, 5120], P(None, 'seq'), may hold values from -0.109375 to 0.109375
- adapter_down: bfloat16 [3072, 32], replicated, may hold values from -0.109375 to 0.109375
- adapter_up_weight: bfloat16 [32, 5120], replicated, may hold values from -1 to 1
- cotangent: bfloat16 [32768, 5120], P(('dp', 'seq')), may hold values from -0.078125 to 0.078125
Outputs:
- mixed: bfloat16 [32768, 5120], P(('dp', 'seq'))
- grad_down: float32 [3072, 32], replicated
- up_weight_gradient: float32 [32, 5120], replicated
The draws below stay inside these ranges and needn't reach their ends.
Inputs may be any that keep to these rules, and one draw needn't show every extreme that they name: `clip_table`: each group is the destination of exactly 2 clips and the source of exactly 2 clips: one has it as both, each other one comes from a different group whose index differs from it in exactly one bit; the bits in which moved clips' groups differ are the same for all groups. Frames run from 1 to 8, heights from 2 to 4, widths are 8 or 16; every group receives one clip of exactly 512 tokens.
All inputs are finite; a program needn't handle non-finite values.
Results may differ from the reference program's by a relative error of at most 0.0094.
Values may be sent and summed in bfloat16 or wider, within the bound.
No kernel may reach another device: no remote copies, remote signals or barrier semaphores. Data moves between devices by JAX's collectives and lax.ppermute only.
A program may use at most 128 MiB of HBM per device.

```python
import math
import jax
import jax.numpy as jnp
from jax import lax

D = 5120
HEAD = 128
HEADS = 24
RANK = 32
CLIPS = 2
FRAMES = 8
TOK_DEV = 128
SRC_DEV = 128
HD = 3072
ROWS = 32768
N_DP = 32
N_SEQ = 8


def draw_clip_table(key, part):
    key = jax.random.fold_in(key, 11)
    keys_all = jax.random.split(key, 7)
    bit_count = N_DP.bit_length() - 1
    groups = jnp.arange(N_DP, dtype=jnp.int32)
    scores = jax.random.randint(keys_all[0], (bit_count,), 0, 4096, dtype=jnp.int32) * bit_count + jnp.arange(bit_count, dtype=jnp.int32)
    ranking = jnp.argsort(scores).astype(jnp.int32)
    chosen = jnp.broadcast_to(ranking[None, :CLIPS - 1], (N_DP, CLIPS - 1))
    partners = jnp.bitwise_xor(groups[:, None], jnp.left_shift(jnp.int32(1), chosen))
    sources = jnp.concatenate([groups[:, None], partners], axis=1)
    targets = jnp.broadcast_to(groups[:, None], (N_DP, CLIPS))
    frames = jax.random.randint(keys_all[1], (N_DP, CLIPS), 1, FRAMES + 1, dtype=jnp.int32)
    height = jax.random.randint(keys_all[2], (N_DP, CLIPS), 2, 5, dtype=jnp.int32)
    widths = N_SEQ * jax.random.randint(keys_all[3], (N_DP, CLIPS), 1, 3, dtype=jnp.int32)
    moved_large = 1 + jax.random.randint(keys_all[4], (N_DP,), 0, CLIPS - 1, dtype=jnp.int32)
    any_large = jax.random.randint(keys_all[5], (N_DP,), 0, CLIPS, dtype=jnp.int32)
    largest = jnp.where(groups % 2 == 0, moved_large, any_large)
    is_large = jnp.arange(CLIPS, dtype=jnp.int32)[None, :] == largest[:, None]
    frames = jnp.where(is_large, FRAMES, frames)
    height = jnp.where(is_large, 4, height)
    widths = jnp.where(is_large, 2 * N_SEQ, widths)
    table_rows = jnp.stack([sources, targets, frames, height, widths], axis=-1).reshape(N_DP * CLIPS, 5)
    shuffle = jax.random.permutation(keys_all[6], N_DP * CLIPS)
    return table_rows[shuffle].astype(jnp.int32)


def draw_attention_inputs(key, part):
    key = jax.random.fold_in(key, 23)
    row_total = N_DP * N_SEQ * SRC_DEV
    feature_total = HEADS * HEAD
    values = jnp.clip(jax.random.normal(key, (3, row_total, feature_total), jnp.float32), -6.0, 6.0)
    return values.astype(jnp.bfloat16)


def levels(key, dims, pieces, low, top_value):
    def one(dim, parts):
        heights = jax.random.uniform(jax.random.fold_in(jax.random.fold_in(key, 6), dim), (parts,), jnp.float32, low / len(pieces), top_value / len(pieces))
        return jnp.repeat(jnp.exp(heights), dims[dim] // parts).reshape((-1,) + (1,) * (len(dims) - dim - 1))

    gain = one(*pieces[0])
    for cut in pieces[1:]:
        gain = gain * one(*cut)
    return gain


def noise(rng, extent, spread, most, pieces=(), kind=jnp.bfloat16):
    result = spread * jax.random.normal(rng, extent, jnp.float32)
    if pieces:
        result = result * levels(rng, extent, pieces, -0.22, 0.18)
    return jnp.clip(result, -most, most).astype(kind)


def setup_inputs(seed: int = 0) -> dict:
    splits = jax.random.split(jax.random.key(seed), 7)
    clip_table = draw_clip_table(jax.random.fold_in(splits[6], 71), 0)
    attention_inputs = draw_attention_inputs(jax.random.fold_in(splits[6], 71), 0)
    out_weight = noise(splits[2], (HD, D), HD ** -0.5, 0.109375, ((1, 8),))
    adapter_down = noise(splits[3], (HD, RANK), HD ** -0.5, 0.109375)
    adapter_up_weight = noise(splits[4], (RANK, D), RANK ** -0.5, 1.0)
    cotangent = noise(splits[5], (ROWS, D), (1.0 / (N_DP * N_SEQ * TOK_DEV) ** 0.5), 0.078125, ((0, 256),))
    return {"clip_table": clip_table, "attention_inputs": attention_inputs, "out_weight": out_weight, "adapter_down": adapter_down, "adapter_up_weight": adapter_up_weight, "cotangent": cotangent}


ADAPTER_SCALE = 2.0

def rope_tables(frame_pos, height_pos, width_pos, head_size):
    sixth_share = head_size // 6
    axis_widths = (head_size - 4 * sixth_share, 2 * sixth_share, 2 * sixth_share)
    angle_parts = []
    for position, axis_width in zip((frame_pos, height_pos, width_pos), axis_widths):
        exponent = jnp.arange(0, axis_width, 2).astype(jnp.float32) / axis_width
        frequency = jnp.power(jnp.float32(10000.0), -exponent)
        angle_parts.append(position.astype(jnp.float32)[:, None] * frequency[None, :])
    angles = jnp.concatenate(angle_parts, axis=1)
    return (jnp.repeat(jnp.cos(angles), 2, axis=1), jnp.repeat(jnp.sin(angles), 2, axis=1))

def clip_layout(clip_table, shard_count):
    source = clip_table[:, 0]
    target = clip_table[:, 1]
    frames = clip_table[:, 2]
    height = clip_table[:, 3]
    widths = clip_table[:, 4]
    portion = (frames * height * widths // shard_count).astype(jnp.int32)
    ordinal = jnp.arange(clip_table.shape[0], dtype=jnp.int32)
    earlier = ordinal[None, :] < ordinal[:, None]
    source_offset = lax.optimization_barrier(jnp.sum(jnp.where(earlier & (source[None, :] == source[:, None]), portion[None, :], 0), axis=1)).astype(jnp.int32)
    target_offset = lax.optimization_barrier(jnp.sum(jnp.where(earlier & (target[None, :] == target[:, None]), portion[None, :], 0), axis=1)).astype(jnp.int32)
    return (source, target, height, widths, portion, source_offset, target_offset)

def rotate_rows(values, cosine_table, sine_table):
    row_count = values.shape[0]
    widened = values.astype(jnp.float32).reshape(row_count, HEADS, HEAD)
    paired = widened.reshape(row_count, HEADS, HEAD // 2, 2)
    swapped = jnp.stack([-paired[..., 1], paired[..., 0]], axis=-1).reshape(row_count, HEADS, HEAD)
    turned = widened * cosine_table[:, None, :] + swapped * sine_table[:, None, :]
    return turned.reshape(row_count, HEADS * HEAD).astype(jnp.bfloat16)

def reference(clip_table, attention_inputs, out_weight, adapter_down, adapter_up_weight, cotangent):
    source, target, height, widths, portion, source_offset, target_offset = clip_layout(clip_table, N_SEQ)
    ordinal = jnp.arange(clip_table.shape[0], dtype=jnp.int32)
    row_index = jnp.arange(TOK_DEV, dtype=jnp.int32)
    seq_index = jnp.arange(N_SEQ, dtype=jnp.int32)
    group_rows = N_SEQ * TOK_DEV
    att_scale = 1.0 / math.sqrt(HEAD)

    def one_group(group_index):
        member = (target[None, :] == group_index) & (row_index[:, None] >= target_offset[None, :]) & (row_index[:, None] < (target_offset + portion)[None, :])
        relative = row_index[:, None] - target_offset[None, :]

        def clip_value(values):
            return lax.optimization_barrier(jnp.sum(jnp.where(member, values, 0), axis=-1)).astype(jnp.int32)
        valid_row = jnp.any(member, axis=1)
        clip_index = clip_value(ordinal[None, :] + 1) - 1
        row_height = jnp.where(valid_row, clip_value(height[None, :]), 1)
        row_width = jnp.where(valid_row, clip_value(widths[None, :]), 1)
        token_index = clip_value(seq_index[:, None, None] * portion[None, None, :] + relative[None, :, :])
        source_row = clip_value((source[None, None, :] * N_SEQ + seq_index[:, None, None]) * SRC_DEV + source_offset[None, None, :] + relative[None, :, :])
        frame_pos = (token_index // (row_height * row_width)[None, :]).reshape(-1)
        height_pos = (token_index // row_width[None, :] % row_height[None, :]).reshape(-1)
        width_pos = (token_index % row_width[None, :]).reshape(-1)
        valid_all = jnp.tile(valid_row, N_SEQ)
        clip_all = jnp.tile(clip_index, N_SEQ)
        taken = jnp.take(attention_inputs, source_row.reshape(-1).astype(jnp.int32), axis=1)
        arranged = jnp.where(valid_all[None, :, None], taken, jnp.zeros((), jnp.bfloat16))
        cosine_table, sine_table = rope_tables(frame_pos, height_pos, width_pos, HEAD)
        queries = rotate_rows(arranged[0], cosine_table, sine_table).astype(jnp.float32).reshape(group_rows, HEADS, HEAD)
        rotated_keys = rotate_rows(arranged[1], cosine_table, sine_table).astype(jnp.float32).reshape(group_rows, HEADS, HEAD)
        head_values = arranged[2].astype(jnp.float32).reshape(group_rows, HEADS, HEAD)
        same_clip = (clip_all[:, None] == clip_all[None, :]) & valid_all[:, None]
        scores = jnp.einsum('qhd,khd->hqk', queries, rotated_keys) * att_scale
        masked = jnp.where(same_clip[None], scores, -1e+30)
        largest = lax.optimization_barrier(jnp.max(masked, axis=2, keepdims=True))
        exponentials = jnp.where(same_clip[None], jnp.exp(masked - largest), 0.0)
        totals = lax.optimization_barrier(jnp.sum(exponentials, axis=2, keepdims=True))
        totals = jnp.where(valid_all[None, :, None], totals, 1.0)
        probabilities = (exponentials / totals).astype(jnp.bfloat16)
        attended = jnp.einsum('hqk,khd->qhd', probabilities.astype(jnp.float32), head_values)
        attended = attended.reshape(group_rows, HEADS * HEAD).astype(jnp.bfloat16)
        projected_output = jnp.dot(attended, out_weight, preferred_element_type=jnp.float32)
        adapter_output = jnp.dot(attended, adapter_down, preferred_element_type=jnp.float32).astype(jnp.bfloat16)
        mixed = (projected_output + ADAPTER_SCALE * jnp.dot(adapter_output, adapter_up_weight, preferred_element_type=jnp.float32)).astype(jnp.bfloat16)
        group_gradient = lax.dynamic_slice_in_dim(cotangent, group_index * group_rows, group_rows, 0)
        hidden_gradient = (ADAPTER_SCALE * jnp.dot(group_gradient, adapter_up_weight.T, preferred_element_type=jnp.float32)).astype(jnp.bfloat16)
        grad_down = jnp.dot(attended.T, hidden_gradient, preferred_element_type=jnp.float32)
        up_weight_gradient = ADAPTER_SCALE * jnp.dot(adapter_output.T, group_gradient, preferred_element_type=jnp.float32)
        return (mixed, grad_down, up_weight_gradient)
    results = lax.map(one_group, jnp.arange(N_DP, dtype=jnp.int32))
    return (results[0].reshape(N_DP * group_rows, D), lax.optimization_barrier(jnp.sum(results[1], axis=0)), lax.optimization_barrier(jnp.sum(results[2], axis=0)))
```

```python
import functools
import math

import jax
import jax.numpy as jnp
import numpy as np
from jax import lax
from jax.experimental import pallas as pl
from jax.experimental.pallas import tpu as pltpu
from jax.sharding import PartitionSpec as P

HEAD = 128
SLOT = 64
ADAPTER_SCALE = 2.0
FAR = (4, 5)
STREAMS = 4
VMEM_BYTES = 56 * 1024 * 1024
F32 = jnp.float32
BF16 = jnp.bfloat16


def contract(left, right, left_dim, right_dim):
    return lax.dot_general(
        left, right, (((left_dim,), (right_dim,)), ((), ())), preferred_element_type=F32
    )


def inverse_frequencies():
    sixth = HEAD // 6
    parts = []
    for width in (HEAD - 4 * sixth, 2 * sixth, 2 * sixth):
        exponent = np.arange(0, width, 2).astype(np.float32) / np.float32(width)
        parts.append(np.power(np.float32(10000.0), -exponent).astype(np.float32))
    return np.broadcast_to(np.repeat(np.concatenate(parts), 2)[None, :], (8, HEAD)).copy()


def iota(shape, dim):
    return lax.broadcasted_iota(jnp.int32, shape, dim)


def my_clips(table, group):
    def step(c, found):
        source, target = table[c, 0], table[c, 1]
        height, width = table[c, 3], table[c, 4]
        portion = table[c, 2] * height * width // 8
        is_source, is_target = source == group, target == group
        chosen = (
            is_source & is_target,
            is_source & jnp.logical_not(is_target),
            is_target & jnp.logical_not(is_source),
        )
        mine = (c, portion, height, width)
        return tuple(
            tuple(jnp.where(hit, new, old) for new, old in zip(mine, clip))
            for hit, clip in zip(chosen, found)
        )

    zero = jnp.int32(0)
    blank = tuple((zero, zero, jnp.int32(1), jnp.int32(1)) for _ in range(3))
    return lax.fori_loop(0, table.shape[0], step, blank)


def placement(shape, row_dim, first, second):
    row = iota(shape, row_dim)
    slot_row = iota(shape, 1 - row_dim)
    in_second = slot_row >= SLOT
    token = jnp.where(in_second, slot_row - SLOT, slot_row)
    offset = jnp.where(in_second, second[0], first[0])
    portion = jnp.where(in_second, second[1], first[1])
    return jnp.where((row == token + offset) & (token < portion), 1.0, 0.0).astype(BF16)


def prepare(place, table, frequency, rows, cotangent, up, *outs):
    stay_out, move_out, to_rows, info = outs
    group, shard = place[0], place[1]
    stay, leave, arrive = my_clips(table, group)
    zero = jnp.int32(0)
    leave_offset = jnp.where(stay[0] < leave[0], stay[1], zero)
    stay_offset = jnp.where(leave[0] < stay[0], leave[1], zero)
    arrive_target = jnp.where(stay[0] < arrive[0], stay[1], zero)
    stay_target = jnp.where(arrive[0] < stay[0], arrive[1], zero)
    info[0] = stay[1]
    info[1] = arrive[1]
    count = rows.shape[1]
    select = placement(
        (2 * SLOT, count), 1, (stay_offset, stay[1]), (leave_offset, leave[1])
    )
    target_rows = placement(
        (cotangent.shape[0], 2 * SLOT), 0, (stay_target, stay[1]), (arrive_target, arrive[1])
    )
    to_rows[...] = target_rows

    shape = (2 * SLOT, HEAD)
    slot_row = iota(shape, 0)
    in_second = slot_row >= SLOT
    token = jnp.where(in_second, slot_row - SLOT, slot_row)
    portion = jnp.where(in_second, leave[1], stay[1])
    height = jnp.where(in_second, leave[2], stay[2]).astype(F32)
    width = jnp.where(in_second, leave[3], stay[3]).astype(F32)
    token = (token + shard * portion).astype(F32)
    row_of = jnp.floor((token + 0.5) / width)
    frame = jnp.floor((token + 0.5) / (height * width))
    sixth = HEAD // 6
    lane = iota(shape, 1)
    position = jnp.where(
        lane < HEAD - 4 * sixth,
        frame,
        jnp.where(lane < HEAD - 2 * sixth, row_of - frame * height, token - row_of * width),
    )
    angle = position * frequency[0:1, :]
    cosine, sine = jnp.cos(angle), jnp.sin(angle)
    even = lane % 2 == 0
    sine_next, sine_last = jnp.where(even, -sine, 0.0), jnp.where(even, 0.0, sine)

    low = (ADAPTER_SCALE * contract(up[...], cotangent[...], 1, 1)).astype(BF16)
    low = contract(low, target_rows, 1, 0).astype(BF16)
    half = low.shape[0] // 2

    width_dev = stay_out.shape[2]
    for k in range(8):
        column = k * width_dev
        for part in range(3):
            placed = contract(select, rows[part, :, pl.ds(column, width_dev)], 1, 0)
            if part < 2:
                turned = []
                for head in range(width_dev // HEAD):
                    lanes = slice(head * HEAD, (head + 1) * HEAD)
                    mine = placed[:, lanes]
                    turned.append(
                        mine * cosine
                        + pltpu.roll(mine, HEAD - 1, 1) * sine_next
                        + pltpu.roll(mine, 1, 1) * sine_last
                    )
                placed = jnp.concatenate(turned, axis=1)
            placed = placed.astype(BF16)
            stay_out[k, part * SLOT : (part + 1) * SLOT, :] = placed[:SLOT]
            start = (3 * k + part) * SLOT
            move_out[start : start + SLOT, :] = placed[SLOT:]
        stay_out[k, 3 * SLOT : 3 * SLOT + half, 0:HEAD] = low[:half]
        stay_out[k, 3 * SLOT : 3 * SLOT + half, HEAD : 2 * HEAD] = low[half:]
        stay_out[k, 3 * SLOT : 3 * SLOT + half, 2 * HEAD :] = jnp.zeros(
            (half, width_dev - 2 * HEAD), BF16
        )


def clip_attention(blocks, portion, store):
    width_dev = blocks[0].shape[1]
    total = 8 * SLOT
    scale = 1.0 / math.sqrt(HEAD)
    valid = lax.rem(iota((total, total), 1), SLOT) < portion
    for head in range(width_dev // HEAD):
        lanes = slice(head * HEAD, (head + 1) * HEAD)
        query, key, value = (
            jnp.concatenate(
                [blocks[k][part * SLOT : (part + 1) * SLOT, lanes] for k in range(8)], axis=0
            )
            for part in range(3)
        )
        scores = jnp.where(valid, contract(query, key, 1, 1) * scale, -1e30)
        largest = jnp.max(scores, axis=1, keepdims=True)
        weights = jnp.exp(scores - largest)
        weights = (weights / jnp.sum(weights, axis=1, keepdims=True)).astype(BF16)
        store(lanes, contract(weights, value, 1, 0).astype(BF16))


def attend_first(info, blocks, out):
    blocks = [blocks.at[k] for k in range(8)]

    def store(lanes, result):
        out[:, lanes] = result

    clip_attention(blocks, info[0], store)


def attend_second(info, first, extras, blocks, out, gradient, second):
    blocks = [blocks.at[k] for k in range(8)]

    def store(lanes, result):
        second[:, lanes] = result

    clip_attention(blocks, info[1], store)
    gradient_sum = jnp.zeros(gradient.shape, F32)
    half = gradient.shape[0] // 2
    for k in range(8):
        rows = slice(k * SLOT, (k + 1) * SLOT)
        out[k, :SLOT, :] = first[rows, :]
        out[k, SLOT:, :] = second[rows, :]
        extra = extras[k, 3 * SLOT : 3 * SLOT + half, :]
        low = jnp.concatenate([extra[:, 0:HEAD], extra[:, HEAD : 2 * HEAD]], axis=0)
        gradient_sum += contract(low, out[k], 1, 0)
    gradient[...] = gradient_sum


def up_gradient(back, to_rows, down, cotangent, down_part, attended, adapted_out, part_out, wide):
    width_dev = back.shape[2]
    for k in range(8):
        attended[:, k * width_dev : (k + 1) * width_dev] = contract(
            to_rows[...], back[k], 1, 0
        ).astype(BF16)
    adapted = contract(down[...], attended[...], 1, 1).astype(BF16)
    adapted_out[...] = adapted
    result = ADAPTER_SCALE * contract(adapted, cotangent[...], 1, 0)
    tiles = result.shape[1] // HEAD
    for j in range(tiles):
        wide[:, j, :] = result[:, j * HEAD : (j + 1) * HEAD]
    for j in range(down_part.shape[1] // HEAD):
        wide[:, tiles + j, :] = down_part[:, j * HEAD : (j + 1) * HEAD]
    for j in range(tiles + down_part.shape[1] // HEAD, wide.shape[1]):
        wide[:, j, :] = jnp.zeros((wide.shape[0], HEAD), F32)
    part_out[...] = wide[...].astype(BF16)


def add_and_repeat(parts, out):
    total = parts[0].astype(F32)
    for i in range(1, parts.shape[0]):
        total += parts[i].astype(F32)
    out[...] = jnp.broadcast_to(total[None], out.shape)


def join_and_repeat(tiles, parts, out, row):
    row[0:tiles, :] = jnp.sum(parts[:, 0:tiles, :], axis=0)
    each = (row.shape[0] - tiles) // 8
    for block in range(8):
        row[tiles + each * block : tiles + each * (block + 1), :] = parts[
            block, tiles : tiles + each, :
        ]
    out[...] = jnp.broadcast_to(row[...].astype(BF16)[None], out.shape)


def spread(parts, up_out, down_out, wide):
    wide[...] = parts[...].astype(F32)
    tiles = up_out.shape[1] // HEAD
    for j in range(tiles):
        up_out[:, j * HEAD : (j + 1) * HEAD] = wide[:, j, :]
    for j in range(down_out.shape[1] // HEAD):
        down_out[:, j * HEAD : (j + 1) * HEAD] = wide[:, tiles + j, :]


def project_own(shard, attended, adapted, up, own, out):
    extra = ADAPTER_SCALE * contract(adapted[...], up[...], 0, 0)
    out[...] = (contract(attended[...], own[...], 1, 0) + extra).astype(BF16)


def project(shard, attended, adapted, up, *refs):
    total = ADAPTER_SCALE * contract(adapted[...], up[...], 0, 0)
    depth = refs[0].shape[0] * refs[0].shape[1]
    for i in range(STREAMS):
        block = refs[i][...].reshape(depth, refs[i].shape[2])
        total += contract(attended[:, i * depth : (i + 1) * depth], block, 1, 0)
    refs[-1][...] = total.astype(BF16)


VM = pl.BlockSpec(memory_space=pltpu.VMEM)
SM = pl.BlockSpec(memory_space=pltpu.SMEM)


def call(kernel, in_specs, out_shapes, out_specs=None, flops=0, size=0, scratch=()):
    return pl.pallas_call(
        kernel,
        in_specs=in_specs,
        out_shape=out_shapes,
        out_specs=out_specs if out_specs is not None else jax.tree.map(lambda _: VM, out_shapes),
        scratch_shapes=scratch,
        compiler_params=pltpu.CompilerParams(vmem_limit_bytes=VMEM_BYTES),
        cost_estimate=pl.CostEstimate(flops=flops, bytes_accessed=size, transcendentals=0),
    )


def body(clip_table, attention_inputs, out_weight, adapter_down, adapter_up_weight, cotangent):
    dp_count, seq_count = lax.axis_size("dp"), lax.axis_size("seq")
    group, shard = lax.axis_index("dp"), lax.axis_index("seq")
    features = attention_inputs.shape[2]
    width_dev = features // seq_count
    feature_dev = out_weight.shape[1]
    rank, model = adapter_up_weight.shape
    rows_dev = cotangent.shape[0]
    place = jnp.stack([group, shard]).astype(jnp.int32)
    struct = jax.ShapeDtypeStruct

    def turn(block, k):
        return lax.ppermute(block, "seq", [(i, (i + k) % seq_count) for i in range(seq_count)])

    weight_rows = features // dp_count
    own_rows = lax.dynamic_slice_in_dim(out_weight, group * weight_rows, weight_rows, 0)
    near = {k: turn(own_rows, -k) for k in range(1, seq_count) if k not in FAR}

    prepared = call(
        prepare,
        [SM, SM, VM, VM, VM, VM],
        [
            struct((seq_count, 3 * SLOT + rank // 2, width_dev), BF16),
            struct((seq_count * 3 * SLOT, width_dev), BF16),
            struct((rows_dev, 2 * SLOT), BF16),
            struct((2,), jnp.int32),
        ],
        [VM] * 3 + [SM],
        flops=10**9,
        size=6 * 10**6,
    )(
        place,
        clip_table,
        jnp.asarray(inverse_frequencies()),
        attention_inputs,
        cotangent,
        adapter_up_weight,
    )
    stay, moving, to_rows, info = prepared

    def exchange(block, axis):
        return lax.all_to_all(block, axis, split_axis=0, concat_axis=0, tiled=True)

    apart = jnp.max(jnp.bitwise_xor(clip_table[:, 0], clip_table[:, 1]))
    bits = dp_count.bit_length() - 1
    branch = sum((apart > (1 << b)).astype(jnp.int32) for b in range(bits - 1))

    def move(bit, moving, stay, above, below):
        moved = lax.ppermute(moving, "dp", [(g, g ^ (1 << bit)) for g in range(dp_count)])
        return moved, exchange(stay, "seq"), turn(above, -1), turn(below, 1)

    moving, *blocks = lax.optimization_barrier((moving, *near.values()))
    blocks = dict(zip(near, blocks))
    moved, stay, *far = lax.switch(
        branch,
        [functools.partial(move, bit) for bit in range(bits)],
        moving,
        stay,
        blocks[FAR[0] - 1],
        blocks[FAR[1] + 1],
    )
    blocks |= dict(zip(FAR, far))
    others = jnp.concatenate([blocks[k] for k in range(1, seq_count)], axis=0)
    others, moved, stay = lax.optimization_barrier((others, moved, stay))
    gathered = lax.all_gather(others, "dp", axis=0, tiled=True)
    gathered = gathered.reshape(dp_count, seq_count - 1, weight_rows, feature_dev)
    moved = exchange(moved.reshape(seq_count, 3 * SLOT, width_dev), "seq")
    first = call(
        attend_first,
        [SM, VM],
        struct((seq_count * SLOT, width_dev), BF16),
        VM,
        flops=10**9,
        size=2 * 10**6,
    )(info, stay)
    attended, down_part = call(
        attend_second,
        [SM] + [VM] * 3,
        [struct((seq_count, 2 * SLOT, width_dev), BF16), struct((rank, width_dev), F32)],
        flops=10**9,
        size=4 * 10**6,
        scratch=[pltpu.VMEM((seq_count * SLOT, width_dev), BF16)],
    )(info, first, stay, moved)
    back = exchange(attended, "seq")

    up_tiles, down_tiles = model // HEAD, features // HEAD
    piece_tiles = -(-(up_tiles + down_tiles // seq_count) // 16) * 16
    attended_rows, adapted, mine = call(
        up_gradient,
        [VM] * 5,
        [
            struct((rows_dev, features), BF16),
            struct((rank, rows_dev), BF16),
            struct((rank, piece_tiles, HEAD), BF16),
        ],
        flops=10**8,
        size=2 * 10**6,
        scratch=[pltpu.VMEM((rank, piece_tiles, HEAD), F32)],
    )(back, to_rows, adapter_down.T, cotangent, down_part)
    mine = exchange(mine, "dp")
    mine = call(add_and_repeat, [VM], struct((seq_count, piece_tiles, HEAD), F32), VM)(mine)

    def whole(shape):
        return pl.BlockSpec(shape, lambda k, s: (0,) * len(shape))

    def mixed_block(first_step):
        return lambda k, s: (0, lax.rem(s[0] + k + first_step, 8))

    begun = pl.pallas_call(
        project_own,
        grid_spec=pltpu.PrefetchScalarGridSpec(
            num_scalar_prefetch=1,
            grid=(1,),
            in_specs=[
                whole((rows_dev, features)),
                whole((rank, rows_dev)),
                pl.BlockSpec((rank, feature_dev), mixed_block(0)),
                whole((features, feature_dev)),
            ],
            out_specs=pl.BlockSpec((rows_dev, feature_dev), mixed_block(0)),
        ),
        out_shape=struct((rows_dev, model), BF16),
        compiler_params=pltpu.CompilerParams(vmem_limit_bytes=VMEM_BYTES),
        cost_estimate=pl.CostEstimate(
            flops=2 * rows_dev * features * feature_dev,
            bytes_accessed=2 * features * feature_dev,
            transcendentals=0,
        ),
    )(place[1:], attended_rows, adapted, adapter_up_weight, out_weight)

    mine = exchange(mine, "seq")
    mine = call(
        functools.partial(join_and_repeat, up_tiles),
        [VM],
        struct((dp_count, up_tiles + down_tiles, HEAD), BF16),
        VM,
        scratch=[pltpu.VMEM((up_tiles + down_tiles, HEAD), F32)],
    )(mine)
    mine, begun, gathered = lax.optimization_barrier((mine, begun, gathered))
    mine = exchange(mine, "dp")
    up_gradient_sum, down_gradient = call(
        spread,
        [VM],
        [struct((rank, model), F32), struct((rank, features), F32)],
        scratch=[pltpu.VMEM((dp_count, up_tiles + down_tiles, HEAD), F32)],
    )(mine)

    mixed = pl.pallas_call(
        project,
        grid_spec=pltpu.PrefetchScalarGridSpec(
            num_scalar_prefetch=1,
            grid=(seq_count - 1,),
            in_specs=[
                whole((rows_dev, features)),
                whole((rank, rows_dev)),
                pl.BlockSpec((rank, feature_dev), mixed_block(1)),
            ]
            + [
                pl.BlockSpec(
                    (dp_count // STREAMS, None, weight_rows, feature_dev),
                    lambda k, s, i=i: (i, k, 0, 0),
                )
                for i in range(STREAMS)
            ]
            + [pl.BlockSpec(memory_space=pl.ANY)],
            out_specs=pl.BlockSpec((rows_dev, feature_dev), mixed_block(1)),
        ),
        out_shape=struct((rows_dev, model), BF16),
        input_output_aliases={4 + STREAMS: 0},
        compiler_params=pltpu.CompilerParams(vmem_limit_bytes=VMEM_BYTES),
        cost_estimate=pl.CostEstimate(
            flops=2 * rows_dev * features * model,
            bytes_accessed=2 * features * model,
            transcendentals=0,
        ),
    )(place[1:], attended_rows, adapted, adapter_up_weight, *[gathered] * STREAMS, begun)
    return (mixed, down_gradient.T, up_gradient_sum)


def solution(mesh):
    in_specs = (P(), P(None, ("dp", "seq"), None), P(None, "seq"), P(), P(), P(("dp", "seq"), None))
    out_specs = (P(("dp", "seq"), None), P(), P())
    return jax.shard_map(body, mesh=mesh, in_specs=in_specs, out_specs=out_specs, check_vma=False)
```

```python
import functools
import math

import jax
import jax.numpy as jnp
import numpy as np
from jax import lax
from jax.experimental import pallas as pl
from jax.experimental.pallas import tpu as pltpu
from jax.sharding import PartitionSpec as P

HEAD = 128
SLOT = 64
ADAPTER_SCALE = 2.0
FAR = (4, 5)
GATHERED = (1, 2, 3, 6, 7, 4, 5)
STREAMS = 4
VMEM_BYTES = 56 * 1024 * 1024
F32 = jnp.float32
BF16 = jnp.bfloat16


def contract(left, right, left_dim, right_dim):
    return lax.dot_general(
        left, right, (((left_dim,), (right_dim,)), ((), ())), preferred_element_type=F32
    )


def inverse_frequencies():
    sixth = HEAD // 6
    parts = []
    for width in (HEAD - 4 * sixth, 2 * sixth, 2 * sixth):
        exponent = np.arange(0, width, 2).astype(np.float32) / np.float32(width)
        parts.append(np.power(np.float32(10000.0), -exponent).astype(np.float32))
    return np.broadcast_to(np.repeat(np.concatenate(parts), 2)[None, :], (8, HEAD)).copy()


def iota(shape, dim):
    return lax.broadcasted_iota(jnp.int32, shape, dim)


def my_clips(table, group):
    def step(c, found):
        source, target = table[0, c], table[1, c]
        height, width = table[3, c], table[4, c]
        portion = table[2, c] * height * width // 8
        is_source, is_target = source == group, target == group
        chosen = (
            is_source & is_target,
            is_source & jnp.logical_not(is_target),
            is_target & jnp.logical_not(is_source),
        )
        mine = (c, portion, height, width)
        return tuple(
            tuple(jnp.where(hit, new, old) for new, old in zip(mine, clip))
            for hit, clip in zip(chosen, found)
        )

    zero = jnp.int32(0)
    blank = tuple((zero, zero, jnp.int32(1), jnp.int32(1)) for _ in range(3))
    return lax.fori_loop(0, table.shape[1], step, blank)


def placement(shape, row_dim, first, second):
    row = iota(shape, row_dim)
    slot_row = iota(shape, 1 - row_dim)
    in_second = slot_row >= SLOT
    token = jnp.where(in_second, slot_row - SLOT, slot_row)
    offset = jnp.where(in_second, second[0], first[0])
    portion = jnp.where(in_second, second[1], first[1])
    return jnp.where((row == token + offset) & (token < portion), 1.0, 0.0).astype(BF16)


def prepare(place, table, frequency, rows, cotangent, up, *outs):
    stay_out, move_out, to_rows, info = outs
    group, shard = place[0], place[1]
    stay, leave, arrive = my_clips(table, group)
    zero = jnp.int32(0)
    leave_offset = jnp.where(stay[0] < leave[0], stay[1], zero)
    stay_offset = jnp.where(leave[0] < stay[0], leave[1], zero)
    arrive_target = jnp.where(stay[0] < arrive[0], stay[1], zero)
    stay_target = jnp.where(arrive[0] < stay[0], arrive[1], zero)
    info[0] = stay[1]
    info[1] = arrive[1]
    count = rows.shape[1]
    select = placement(
        (2 * SLOT, count), 1, (stay_offset, stay[1]), (leave_offset, leave[1])
    )
    target_rows = placement(
        (cotangent.shape[0], 2 * SLOT), 0, (stay_target, stay[1]), (arrive_target, arrive[1])
    )
    to_rows[...] = target_rows

    shape = (2 * SLOT, HEAD)
    slot_row = iota(shape, 0)
    in_second = slot_row >= SLOT
    token = jnp.where(in_second, slot_row - SLOT, slot_row)
    portion = jnp.where(in_second, leave[1], stay[1])
    height = jnp.where(in_second, leave[2], stay[2]).astype(F32)
    width = jnp.where(in_second, leave[3], stay[3]).astype(F32)
    token = (token + shard * portion).astype(F32)
    row_of = jnp.floor((token + 0.5) / width)
    frame = jnp.floor((token + 0.5) / (height * width))
    sixth = HEAD // 6
    lane = iota(shape, 1)
    position = jnp.where(
        lane < HEAD - 4 * sixth,
        frame,
        jnp.where(lane < HEAD - 2 * sixth, row_of - frame * height, token - row_of * width),
    )
    angle = position * frequency[0:1, :]
    cosine, sine = jnp.cos(angle), jnp.sin(angle)
    even = lane % 2 == 0
    sine_next, sine_last = jnp.where(even, -sine, 0.0), jnp.where(even, 0.0, sine)

    low = (ADAPTER_SCALE * contract(up[...], cotangent[...], 1, 1)).astype(BF16)
    low = contract(low, target_rows, 1, 0).astype(BF16)
    half = low.shape[0] // 2

    width_dev = stay_out.shape[2]
    for k in range(8):
        column = k * width_dev
        for part in range(3):
            placed = contract(select, rows[part, :, pl.ds(column, width_dev)], 1, 0)
            if part < 2:
                turned = []
                for head in range(width_dev // HEAD):
                    lanes = slice(head * HEAD, (head + 1) * HEAD)
                    mine = placed[:, lanes]
                    turned.append(
                        mine * cosine
                        + pltpu.roll(mine, HEAD - 1, 1) * sine_next
                        + pltpu.roll(mine, 1, 1) * sine_last
                    )
                placed = jnp.concatenate(turned, axis=1)
            placed = placed.astype(BF16)
            stay_out[k, part * SLOT : (part + 1) * SLOT, :] = placed[:SLOT]
            start = (3 * k + part) * SLOT
            move_out[start : start + SLOT, :] = placed[SLOT:]
        stay_out[k, 3 * SLOT : 3 * SLOT + half, 0:HEAD] = low[:half]
        stay_out[k, 3 * SLOT : 3 * SLOT + half, HEAD : 2 * HEAD] = low[half:]
        stay_out[k, 3 * SLOT : 3 * SLOT + half, 2 * HEAD :] = jnp.zeros(
            (half, width_dev - 2 * HEAD), BF16
        )


def clip_attention(blocks, portion, store):
    width_dev = blocks[0].shape[1]
    total = 8 * SLOT
    scale = 1.0 / math.sqrt(HEAD)
    valid = lax.rem(iota((total, total), 1), SLOT) < portion
    for head in range(width_dev // HEAD):
        lanes = slice(head * HEAD, (head + 1) * HEAD)
        query, key, value = (
            jnp.concatenate(
                [blocks[k][part * SLOT : (part + 1) * SLOT, lanes] for k in range(8)], axis=0
            )
            for part in range(3)
        )
        scores = jnp.where(valid, contract(query, key, 1, 1) * scale, -1e30)
        largest = jnp.max(scores, axis=1, keepdims=True)
        weights = jnp.exp(scores - largest)
        weights = (weights / jnp.sum(weights, axis=1, keepdims=True)).astype(BF16)
        store(lanes, contract(weights, value, 1, 0).astype(BF16))


def attend_first(info, blocks, out):
    blocks = [blocks.at[k] for k in range(8)]

    def store(lanes, result):
        out[:, lanes] = result

    clip_attention(blocks, info[0], store)


def attend_second(info, first, extras, blocks, out, gradient, second):
    blocks = [blocks.at[k] for k in range(8)]

    def store(lanes, result):
        second[:, lanes] = result

    clip_attention(blocks, info[1], store)
    gradient_sum = jnp.zeros(gradient.shape, F32)
    half = gradient.shape[0] // 2
    for k in range(8):
        rows = slice(k * SLOT, (k + 1) * SLOT)
        out[k, :SLOT, :] = first[rows, :]
        out[k, SLOT:, :] = second[rows, :]
        extra = extras[k, 3 * SLOT : 3 * SLOT + half, :]
        low = jnp.concatenate([extra[:, 0:HEAD], extra[:, HEAD : 2 * HEAD]], axis=0)
        gradient_sum += contract(low, out[k], 1, 0)
    gradient[...] = gradient_sum


def up_gradient(back, to_rows, down, cotangent, down_part, attended, adapted_out, part_out, wide):
    width_dev = back.shape[2]
    for k in range(8):
        attended[:, k * width_dev : (k + 1) * width_dev] = contract(
            to_rows[...], back[k], 1, 0
        ).astype(BF16)
    adapted = contract(down[...], attended[...], 1, 1).astype(BF16)
    adapted_out[...] = adapted
    result = ADAPTER_SCALE * contract(adapted, cotangent[...], 1, 0)
    tiles = result.shape[1] // HEAD
    for j in range(tiles):
        wide[:, j, :] = result[:, j * HEAD : (j + 1) * HEAD]
    for j in range(down_part.shape[1] // HEAD):
        wide[:, tiles + j, :] = down_part[:, j * HEAD : (j + 1) * HEAD]
    for j in range(tiles + down_part.shape[1] // HEAD, wide.shape[1]):
        wide[:, j, :] = jnp.zeros((wide.shape[0], HEAD), F32)
    part_out[...] = wide[...].astype(BF16)


def add_and_repeat(parts, out):
    total = parts[0].astype(F32)
    for i in range(1, parts.shape[0]):
        total += parts[i].astype(F32)
    out[...] = jnp.broadcast_to(total[None], out.shape)


def join_and_repeat(tiles, parts, out, row):
    row[0:tiles, :] = jnp.sum(parts[:, 0:tiles, :], axis=0)
    each = (row.shape[0] - tiles) // 8
    for block in range(8):
        row[tiles + each * block : tiles + each * (block + 1), :] = parts[
            block, tiles : tiles + each, :
        ]
    out[...] = jnp.broadcast_to(row[...].astype(BF16)[None], out.shape)


def spread(parts, up_out, down_out, wide):
    wide[...] = parts[...].astype(F32)
    tiles = up_out.shape[1] // HEAD
    for j in range(tiles):
        up_out[:, j * HEAD : (j + 1) * HEAD] = wide[:, j, :]
    for j in range(down_out.shape[1] // HEAD):
        down_out[:, j * HEAD : (j + 1) * HEAD] = wide[:, tiles + j, :]


def project_own(shard, attended, adapted, up, own, out):
    extra = ADAPTER_SCALE * contract(adapted[...], up[...], 0, 0)
    out[...] = (contract(attended[...], own[...], 1, 0) + extra).astype(BF16)


def project(shard, attended, adapted, up, *refs):
    total = ADAPTER_SCALE * contract(adapted[...], up[...], 0, 0)
    depth = refs[0].shape[0] * refs[0].shape[1]
    for i in range(STREAMS):
        block = refs[i][...].reshape(depth, refs[i].shape[2])
        total += contract(attended[:, i * depth : (i + 1) * depth], block, 1, 0)
    refs[-1][...] = total.astype(BF16)


VM = pl.BlockSpec(memory_space=pltpu.VMEM)
SM = pl.BlockSpec(memory_space=pltpu.SMEM)


def call(kernel, in_specs, out_shapes, out_specs=None, flops=0, size=0, scratch=()):
    return pl.pallas_call(
        kernel,
        in_specs=in_specs,
        out_shape=out_shapes,
        out_specs=out_specs if out_specs is not None else jax.tree.map(lambda _: VM, out_shapes),
        scratch_shapes=scratch,
        compiler_params=pltpu.CompilerParams(vmem_limit_bytes=VMEM_BYTES),
        cost_estimate=pl.CostEstimate(flops=flops, bytes_accessed=size, transcendentals=0),
    )


def body(clip_table, attention_inputs, out_weight, adapter_down, adapter_up_weight, cotangent):
    dp_count, seq_count = lax.axis_size("dp"), lax.axis_size("seq")
    group, shard = lax.axis_index("dp"), lax.axis_index("seq")
    features = attention_inputs.shape[2]
    width_dev = features // seq_count
    feature_dev = out_weight.shape[1]
    rank, model = adapter_up_weight.shape
    rows_dev = cotangent.shape[0]
    place = jnp.stack([group, shard]).astype(jnp.int32)
    struct = jax.ShapeDtypeStruct

    def turn(block, k):
        return lax.ppermute(block, "seq", [(i, (i + k) % seq_count) for i in range(seq_count)])

    weight_rows = features // dp_count
    own_rows = lax.dynamic_slice_in_dim(out_weight, group * weight_rows, weight_rows, 0)
    near = {k: turn(own_rows, -k) for k in range(1, seq_count) if k not in FAR}

    prepared = call(
        prepare,
        [SM, SM, VM, VM, VM, VM],
        [
            struct((seq_count, 3 * SLOT + rank // 2, width_dev), BF16),
            struct((seq_count * 3 * SLOT, width_dev), BF16),
            struct((rows_dev, 2 * SLOT), BF16),
            struct((2,), jnp.int32),
        ],
        [VM] * 3 + [SM],
        flops=10**9,
        size=6 * 10**6,
    )(
        place,
        clip_table.T,
        jnp.asarray(inverse_frequencies()),
        attention_inputs,
        cotangent,
        adapter_up_weight,
    )
    stay, moving, to_rows, info = prepared

    def exchange(block, axis):
        return lax.all_to_all(block, axis, split_axis=0, concat_axis=0, tiled=True)

    apart = jnp.bitwise_xor(clip_table[:, 0], clip_table[:, 1])
    bits = dp_count.bit_length() - 1
    branch = jnp.max(sum((apart > (1 << b)).astype(jnp.int32) for b in range(bits - 1)))

    def move(bit, moving, stay, above, below):
        moved = lax.ppermute(moving, "dp", [(g, g ^ (1 << bit)) for g in range(dp_count)])
        return moved, exchange(stay, "seq"), turn(above, -1), turn(below, 1)

    moving, *blocks = lax.optimization_barrier((moving, *near.values()))
    blocks = dict(zip(near, blocks))
    moved, stay, *far = lax.switch(
        branch,
        [functools.partial(move, bit) for bit in range(bits)],
        moving,
        stay,
        blocks[FAR[0] - 1],
        blocks[FAR[1] + 1],
    )
    blocks |= dict(zip(FAR, far))
    others = jnp.concatenate([blocks[k] for k in GATHERED], axis=0)
    others, moved, stay = lax.optimization_barrier((others, moved, stay))
    gathered = lax.all_gather(others, "dp", axis=0, tiled=True)
    gathered = gathered.reshape(dp_count, seq_count - 1, weight_rows, feature_dev)
    moved = exchange(moved.reshape(seq_count, 3 * SLOT, width_dev), "seq")
    first = call(
        attend_first,
        [SM, VM],
        struct((seq_count * SLOT, width_dev), BF16),
        VM,
        flops=10**9,
        size=2 * 10**6,
    )(info, stay)
    attended, down_part = call(
        attend_second,
        [SM] + [VM] * 3,
        [struct((seq_count, 2 * SLOT, width_dev), BF16), struct((rank, width_dev), F32)],
        flops=10**9,
        size=4 * 10**6,
        scratch=[pltpu.VMEM((seq_count * SLOT, width_dev), BF16)],
    )(info, first, stay, moved)
    back = exchange(attended, "seq")

    up_tiles, down_tiles = model // HEAD, features // HEAD
    piece_tiles = -(-(up_tiles + down_tiles // seq_count) // 16) * 16
    attended_rows, adapted, mine = call(
        up_gradient,
        [VM] * 5,
        [
            struct((rows_dev, features), BF16),
            struct((rank, rows_dev), BF16),
            struct((rank, piece_tiles, HEAD), BF16),
        ],
        flops=10**8,
        size=2 * 10**6,
        scratch=[pltpu.VMEM((rank, piece_tiles, HEAD), F32)],
    )(back, to_rows, adapter_down.T, cotangent, down_part)
    mine = exchange(mine, "dp")
    mine = call(add_and_repeat, [VM], struct((seq_count, piece_tiles, HEAD), F32), VM)(mine)

    def whole(shape):
        return pl.BlockSpec(shape, lambda k, s: (0,) * len(shape))

    def own_block(k, s):
        return (0, s[0])

    def gathered_block(k, s):
        away = jnp.where(k < 3, k + 1, jnp.where(k < 5, k + 3, k - 1))
        return (0, lax.rem(s[0] + away, 8))

    begun = pl.pallas_call(
        project_own,
        grid_spec=pltpu.PrefetchScalarGridSpec(
            num_scalar_prefetch=1,
            grid=(1,),
            in_specs=[
                whole((rows_dev, features)),
                whole((rank, rows_dev)),
                pl.BlockSpec((rank, feature_dev), own_block),
                whole((features, feature_dev)),
            ],
            out_specs=pl.BlockSpec((rows_dev, feature_dev), own_block),
        ),
        out_shape=struct((rows_dev, model), BF16),
        compiler_params=pltpu.CompilerParams(vmem_limit_bytes=VMEM_BYTES),
        cost_estimate=pl.CostEstimate(
            flops=2 * rows_dev * features * feature_dev,
            bytes_accessed=2 * features * feature_dev,
            transcendentals=0,
        ),
    )(place[1:], attended_rows, adapted, adapter_up_weight, out_weight)

    mine = exchange(mine, "seq")
    mine = call(
        functools.partial(join_and_repeat, up_tiles),
        [VM],
        struct((dp_count, up_tiles + down_tiles, HEAD), BF16),
        VM,
        scratch=[pltpu.VMEM((up_tiles + down_tiles, HEAD), F32)],
    )(mine)
    mine, begun, gathered = lax.optimization_barrier((mine, begun, gathered))
    mine = exchange(mine, "dp")
    up_gradient_sum, down_gradient = call(
        spread,
        [VM],
        [struct((rank, model), F32), struct((rank, features), F32)],
        scratch=[pltpu.VMEM((dp_count, up_tiles + down_tiles, HEAD), F32)],
    )(mine)

    mixed = pl.pallas_call(
        project,
        grid_spec=pltpu.PrefetchScalarGridSpec(
            num_scalar_prefetch=1,
            grid=(seq_count - 1,),
            in_specs=[
                whole((rows_dev, features)),
                whole((rank, rows_dev)),
                pl.BlockSpec((rank, feature_dev), gathered_block),
            ]
            + [
                pl.BlockSpec(
                    (dp_count // STREAMS, None, weight_rows, feature_dev),
                    lambda k, s, i=i: (i, k, 0, 0),
                )
                for i in range(STREAMS)
            ]
            + [pl.BlockSpec(memory_space=pl.ANY)],
            out_specs=pl.BlockSpec((rows_dev, feature_dev), gathered_block),
        ),
        out_shape=struct((rows_dev, model), BF16),
        input_output_aliases={4 + STREAMS: 0},
        compiler_params=pltpu.CompilerParams(vmem_limit_bytes=VMEM_BYTES),
        cost_estimate=pl.CostEstimate(
            flops=2 * rows_dev * features * model,
            bytes_accessed=2 * features * model,
            transcendentals=0,
        ),
    )(place[1:], attended_rows, adapted, adapter_up_weight, *[gathered] * STREAMS, begun)
    return (mixed, down_gradient.T, up_gradient_sum)


def solution(mesh):
    in_specs = (P(), P(None, ("dp", "seq"), None), P(None, "seq"), P(), P(), P(("dp", "seq"), None))
    out_specs = (P(("dp", "seq"), None), P(), P())
    return jax.shard_map(body, mesh=mesh, in_specs=in_specs, out_specs=out_specs, check_vma=False)
```

```python
import functools
import math

import jax
import jax.numpy as jnp
import numpy as np
from jax import lax
from jax.experimental import pallas as pl
from jax.experimental.pallas import tpu as pltpu
from jax.sharding import PartitionSpec as P

HEAD = 128
SLOT = 64
ADAPTER_SCALE = 2.0
FAR = (3, 4, 5)
STREAMS = 4
VMEM_BYTES = 56 * 1024 * 1024
F32 = jnp.float32
BF16 = jnp.bfloat16


def contract(left, right, left_dim, right_dim):
    return lax.dot_general(
        left, right, (((left_dim,), (right_dim,)), ((), ())), preferred_element_type=F32
    )


def inverse_frequencies():
    sixth = HEAD // 6
    parts = []
    for width in (HEAD - 4 * sixth, 2 * sixth, 2 * sixth):
        exponent = np.arange(0, width, 2).astype(np.float32) / np.float32(width)
        parts.append(np.power(np.float32(10000.0), -exponent).astype(np.float32))
    return np.broadcast_to(np.repeat(np.concatenate(parts), 2)[None, :], (8, HEAD)).copy()


def iota(shape, dim):
    return lax.broadcasted_iota(jnp.int32, shape, dim)


def my_clips(table, group):
    def step(c, found):
        source, target = table[0, c], table[1, c]
        height, width = table[3, c], table[4, c]
        portion = table[2, c] * height * width // 8
        is_source, is_target = source == group, target == group
        chosen = (
            is_source & is_target,
            is_source & jnp.logical_not(is_target),
            is_target & jnp.logical_not(is_source),
        )
        mine = (c, portion, height, width)
        return tuple(
            tuple(jnp.where(hit, new, old) for new, old in zip(mine, clip))
            for hit, clip in zip(chosen, found)
        )

    zero = jnp.int32(0)
    blank = tuple((zero, zero, jnp.int32(1), jnp.int32(1)) for _ in range(3))
    return lax.fori_loop(0, table.shape[1], step, blank)


def placement(shape, row_dim, first, second):
    row = iota(shape, row_dim)
    slot_row = iota(shape, 1 - row_dim)
    in_second = slot_row >= SLOT
    token = jnp.where(in_second, slot_row - SLOT, slot_row)
    offset = jnp.where(in_second, second[0], first[0])
    portion = jnp.where(in_second, second[1], first[1])
    return jnp.where((row == token + offset) & (token < portion), 1.0, 0.0).astype(BF16)


def prepare(place, table, frequency, rows, cotangent, up, *outs):
    stay_out, move_out, to_rows, info = outs
    group, shard = place[0], place[1]
    stay, leave, arrive = my_clips(table, group)
    zero = jnp.int32(0)
    leave_offset = jnp.where(stay[0] < leave[0], stay[1], zero)
    stay_offset = jnp.where(leave[0] < stay[0], leave[1], zero)
    arrive_target = jnp.where(stay[0] < arrive[0], stay[1], zero)
    stay_target = jnp.where(arrive[0] < stay[0], arrive[1], zero)
    info[0] = stay[1]
    info[1] = arrive[1]
    count = rows.shape[1]
    select = placement(
        (2 * SLOT, count), 1, (stay_offset, stay[1]), (leave_offset, leave[1])
    )
    target_rows = placement(
        (cotangent.shape[0], 2 * SLOT), 0, (stay_target, stay[1]), (arrive_target, arrive[1])
    )
    to_rows[...] = target_rows

    shape = (2 * SLOT, HEAD)
    slot_row = iota(shape, 0)
    in_second = slot_row >= SLOT
    token = jnp.where(in_second, slot_row - SLOT, slot_row)
    portion = jnp.where(in_second, leave[1], stay[1])
    height = jnp.where(in_second, leave[2], stay[2]).astype(F32)
    width = jnp.where(in_second, leave[3], stay[3]).astype(F32)
    token = (token + shard * portion).astype(F32)
    row_of = jnp.floor((token + 0.5) / width)
    frame = jnp.floor((token + 0.5) / (height * width))
    sixth = HEAD // 6
    lane = iota(shape, 1)
    position = jnp.where(
        lane < HEAD - 4 * sixth,
        frame,
        jnp.where(lane < HEAD - 2 * sixth, row_of - frame * height, token - row_of * width),
    )
    angle = position * frequency[0:1, :]
    cosine, sine = jnp.cos(angle), jnp.sin(angle)
    even = lane % 2 == 0
    sine_next, sine_last = jnp.where(even, -sine, 0.0), jnp.where(even, 0.0, sine)

    low = (ADAPTER_SCALE * contract(up[...], cotangent[...], 1, 1)).astype(BF16)
    low = contract(low, target_rows, 1, 0).astype(BF16)
    half = low.shape[0] // 2

    width_dev = stay_out.shape[2]
    for k in range(8):
        column = k * width_dev
        for part in range(3):
            placed = contract(select, rows[part, :, pl.ds(column, width_dev)], 1, 0)
            if part < 2:
                turned = []
                for head in range(width_dev // HEAD):
                    lanes = slice(head * HEAD, (head + 1) * HEAD)
                    mine = placed[:, lanes]
                    turned.append(
                        mine * cosine
                        + pltpu.roll(mine, HEAD - 1, 1) * sine_next
                        + pltpu.roll(mine, 1, 1) * sine_last
                    )
                placed = jnp.concatenate(turned, axis=1)
            placed = placed.astype(BF16)
            stay_out[k, part * SLOT : (part + 1) * SLOT, :] = placed[:SLOT]
            start = (3 * k + part) * SLOT
            move_out[start : start + SLOT, :] = placed[SLOT:]
        stay_out[k, 3 * SLOT : 3 * SLOT + half, 0:HEAD] = low[:half]
        stay_out[k, 3 * SLOT : 3 * SLOT + half, HEAD : 2 * HEAD] = low[half:]
        stay_out[k, 3 * SLOT : 3 * SLOT + half, 2 * HEAD :] = jnp.zeros(
            (half, width_dev - 2 * HEAD), BF16
        )


def clip_attention(blocks, portion, store):
    width_dev = blocks[0].shape[1]
    total = 8 * SLOT
    scale = 1.0 / math.sqrt(HEAD)
    valid = lax.rem(iota((total, total), 1), SLOT) < portion
    for head in range(width_dev // HEAD):
        lanes = slice(head * HEAD, (head + 1) * HEAD)
        query, key, value = (
            jnp.concatenate(
                [blocks[k][part * SLOT : (part + 1) * SLOT, lanes] for k in range(8)], axis=0
            )
            for part in range(3)
        )
        scores = jnp.where(valid, contract(query, key, 1, 1) * scale, -1e30)
        largest = jnp.max(scores, axis=1, keepdims=True)
        weights = jnp.exp(scores - largest)
        weights = (weights / jnp.sum(weights, axis=1, keepdims=True)).astype(BF16)
        store(lanes, contract(weights, value, 1, 0).astype(BF16))


def attend_first(info, blocks, out):
    blocks = [blocks.at[k] for k in range(8)]

    def store(lanes, result):
        out[:, lanes] = result

    clip_attention(blocks, info[0], store)


def attend_second(info, first, extras, blocks, out, gradient, second):
    blocks = [blocks.at[k] for k in range(8)]

    def store(lanes, result):
        second[:, lanes] = result

    clip_attention(blocks, info[1], store)
    gradient_sum = jnp.zeros(gradient.shape, F32)
    half = gradient.shape[0] // 2
    for k in range(8):
        rows = slice(k * SLOT, (k + 1) * SLOT)
        out[k, :SLOT, :] = first[rows, :]
        out[k, SLOT:, :] = second[rows, :]
        extra = extras[k, 3 * SLOT : 3 * SLOT + half, :]
        low = jnp.concatenate([extra[:, 0:HEAD], extra[:, HEAD : 2 * HEAD]], axis=0)
        gradient_sum += contract(low, out[k], 1, 0)
    gradient[...] = gradient_sum


def up_gradient(back, to_rows, down, cotangent, down_part, attended, adapted_out, part_out, wide):
    width_dev = back.shape[2]
    for k in range(8):
        attended[:, k * width_dev : (k + 1) * width_dev] = contract(
            to_rows[...], back[k], 1, 0
        ).astype(BF16)
    adapted = contract(down[...], attended[...], 1, 1).astype(BF16)
    adapted_out[...] = adapted
    result = ADAPTER_SCALE * contract(adapted, cotangent[...], 1, 0)
    tiles = result.shape[1] // HEAD
    for j in range(tiles):
        wide[:, j, :] = result[:, j * HEAD : (j + 1) * HEAD]
    for j in range(down_part.shape[1] // HEAD):
        wide[:, tiles + j, :] = down_part[:, j * HEAD : (j + 1) * HEAD]
    for j in range(tiles + down_part.shape[1] // HEAD, wide.shape[1]):
        wide[:, j, :] = jnp.zeros((wide.shape[0], HEAD), F32)
    part_out[...] = wide[...].astype(BF16)


def add_and_repeat(parts, out):
    total = parts[0].astype(F32)
    for i in range(1, parts.shape[0]):
        total += parts[i].astype(F32)
    out[...] = jnp.broadcast_to(total[None], out.shape)


def join_and_repeat(tiles, parts, out, row):
    row[0:tiles, :] = jnp.sum(parts[:, 0:tiles, :], axis=0)
    each = (row.shape[0] - tiles) // 8
    for block in range(8):
        row[tiles + each * block : tiles + each * (block + 1), :] = parts[
            block, tiles : tiles + each, :
        ]
    out[...] = jnp.broadcast_to(row[...].astype(BF16)[None], out.shape)


def spread(parts, up_out, down_out, wide):
    wide[...] = parts[...].astype(F32)
    tiles = up_out.shape[1] // HEAD
    for j in range(tiles):
        up_out[:, j * HEAD : (j + 1) * HEAD] = wide[:, j, :]
    for j in range(down_out.shape[1] // HEAD):
        down_out[:, j * HEAD : (j + 1) * HEAD] = wide[:, tiles + j, :]


def project_own(shard, attended, adapted, up, own, out):
    extra = ADAPTER_SCALE * contract(adapted[...], up[...], 0, 0)
    out[...] = (contract(attended[...], own[...], 1, 0) + extra).astype(BF16)


def project(shard, attended, adapted, up, *refs):
    total = ADAPTER_SCALE * contract(adapted[...], up[...], 0, 0)
    depth = refs[0].shape[0] * refs[0].shape[1]
    for i in range(STREAMS):
        block = refs[i][...].reshape(depth, refs[i].shape[2])
        total += contract(attended[:, i * depth : (i + 1) * depth], block, 1, 0)
    refs[-1][...] = total.astype(BF16)


VM = pl.BlockSpec(memory_space=pltpu.VMEM)
SM = pl.BlockSpec(memory_space=pltpu.SMEM)


def call(kernel, in_specs, out_shapes, out_specs=None, flops=0, size=0, scratch=()):
    return pl.pallas_call(
        kernel,
        in_specs=in_specs,
        out_shape=out_shapes,
        out_specs=out_specs if out_specs is not None else jax.tree.map(lambda _: VM, out_shapes),
        scratch_shapes=scratch,
        compiler_params=pltpu.CompilerParams(vmem_limit_bytes=VMEM_BYTES),
        cost_estimate=pl.CostEstimate(flops=flops, bytes_accessed=size, transcendentals=0),
    )


def body(clip_table, attention_inputs, out_weight, adapter_down, adapter_up_weight, cotangent):
    dp_count, seq_count = lax.axis_size("dp"), lax.axis_size("seq")
    group, shard = lax.axis_index("dp"), lax.axis_index("seq")
    features = attention_inputs.shape[2]
    width_dev = features // seq_count
    feature_dev = out_weight.shape[1]
    rank, model = adapter_up_weight.shape
    rows_dev = cotangent.shape[0]
    place = jnp.stack([group, shard]).astype(jnp.int32)
    struct = jax.ShapeDtypeStruct

    def turn(block, k):
        return lax.ppermute(block, "seq", [(i, (i + k) % seq_count) for i in range(seq_count)])

    weight_rows = features // dp_count
    own_rows = lax.dynamic_slice_in_dim(out_weight, group * weight_rows, weight_rows, 0)
    near = {k: turn(own_rows, -k) for k in range(1, seq_count) if k not in FAR}

    prepared = call(
        prepare,
        [SM, SM, VM, VM, VM, VM],
        [
            struct((seq_count, 3 * SLOT + rank // 2, width_dev), BF16),
            struct((seq_count * 3 * SLOT, width_dev), BF16),
            struct((rows_dev, 2 * SLOT), BF16),
            struct((2,), jnp.int32),
        ],
        [VM] * 3 + [SM],
        flops=10**9,
        size=6 * 10**6,
    )(
        place,
        clip_table.T,
        jnp.asarray(inverse_frequencies()),
        attention_inputs,
        cotangent,
        adapter_up_weight,
    )
    stay, moving, to_rows, info = prepared

    def exchange(block, axis):
        return lax.all_to_all(block, axis, split_axis=0, concat_axis=0, tiled=True)

    apart = jnp.bitwise_xor(clip_table[:, 0], clip_table[:, 1])
    bits = dp_count.bit_length() - 1
    branch = jnp.max(sum((apart > (1 << b)).astype(jnp.int32) for b in range(bits - 1)))

    def move(bit, moving, stay, pair, below):
        moved = lax.ppermute(moving, "dp", [(g, g ^ (1 << bit)) for g in range(dp_count)])
        return moved, exchange(stay, "seq"), turn(pair, -2), turn(below, 1)

    pair = jnp.concatenate([near[1], near[2]], axis=0)
    moving, pair, *blocks = lax.optimization_barrier((moving, pair, *near.values()))
    blocks = dict(zip(near, blocks))
    moved, stay, *far = lax.switch(
        branch,
        [functools.partial(move, bit) for bit in range(bits)],
        moving,
        stay,
        pair,
        blocks[6],
    )
    others = jnp.concatenate([pair, blocks[6], blocks[7], *far], axis=0)
    others, moved, stay = lax.optimization_barrier((others, moved, stay))
    gathered = lax.all_gather(others, "dp", axis=0, tiled=True)
    gathered = gathered.reshape(dp_count, seq_count - 1, weight_rows, feature_dev)
    moved = exchange(moved.reshape(seq_count, 3 * SLOT, width_dev), "seq")
    first = call(
        attend_first,
        [SM, VM],
        struct((seq_count * SLOT, width_dev), BF16),
        VM,
        flops=10**9,
        size=2 * 10**6,
    )(info, stay)
    attended, down_part = call(
        attend_second,
        [SM] + [VM] * 3,
        [struct((seq_count, 2 * SLOT, width_dev), BF16), struct((rank, width_dev), F32)],
        flops=10**9,
        size=4 * 10**6,
        scratch=[pltpu.VMEM((seq_count * SLOT, width_dev), BF16)],
    )(info, first, stay, moved)
    back = exchange(attended, "seq")

    up_tiles, down_tiles = model // HEAD, features // HEAD
    piece_tiles = -(-(up_tiles + down_tiles // seq_count) // 16) * 16
    attended_rows, adapted, mine = call(
        up_gradient,
        [VM] * 5,
        [
            struct((rows_dev, features), BF16),
            struct((rank, rows_dev), BF16),
            struct((rank, piece_tiles, HEAD), BF16),
        ],
        flops=10**8,
        size=2 * 10**6,
        scratch=[pltpu.VMEM((rank, piece_tiles, HEAD), F32)],
    )(back, to_rows, adapter_down.T, cotangent, down_part)
    mine = exchange(mine, "dp")
    mine = call(add_and_repeat, [VM], struct((seq_count, piece_tiles, HEAD), F32), VM)(mine)

    def whole(shape):
        return pl.BlockSpec(shape, lambda k, s: (0,) * len(shape))

    def own_block(k, s):
        return (0, s[0])

    def gathered_block(k, s):
        away = jnp.where(k < 2, k + 1, jnp.where(k < 4, k + 4, k - 1))
        return (0, lax.rem(s[0] + away, 8))

    begun = pl.pallas_call(
        project_own,
        grid_spec=pltpu.PrefetchScalarGridSpec(
            num_scalar_prefetch=1,
            grid=(1,),
            in_specs=[
                whole((rows_dev, features)),
                whole((rank, rows_dev)),
                pl.BlockSpec((rank, feature_dev), own_block),
                whole((features, feature_dev)),
            ],
            out_specs=pl.BlockSpec((rows_dev, feature_dev), own_block),
        ),
        out_shape=struct((rows_dev, model), BF16),
        compiler_params=pltpu.CompilerParams(vmem_limit_bytes=VMEM_BYTES),
        cost_estimate=pl.CostEstimate(
            flops=2 * rows_dev * features * feature_dev,
            bytes_accessed=2 * features * feature_dev,
            transcendentals=0,
        ),
    )(place[1:], attended_rows, adapted, adapter_up_weight, out_weight)

    mine = exchange(mine, "seq")
    mine = call(
        functools.partial(join_and_repeat, up_tiles),
        [VM],
        struct((dp_count, up_tiles + down_tiles, HEAD), BF16),
        VM,
        scratch=[pltpu.VMEM((up_tiles + down_tiles, HEAD), F32)],
    )(mine)
    mine, begun, gathered = lax.optimization_barrier((mine, begun, gathered))
    mine = exchange(mine, "dp")
    up_gradient_sum, down_gradient = call(
        spread,
        [VM],
        [struct((rank, model), F32), struct((rank, features), F32)],
        scratch=[pltpu.VMEM((dp_count, up_tiles + down_tiles, HEAD), F32)],
    )(mine)

    mixed = pl.pallas_call(
        project,
        grid_spec=pltpu.PrefetchScalarGridSpec(
            num_scalar_prefetch=1,
            grid=(seq_count - 1,),
            in_specs=[
                whole((rows_dev, features)),
                whole((rank, rows_dev)),
                pl.BlockSpec((rank, feature_dev), gathered_block),
            ]
            + [
                pl.BlockSpec(
                    (dp_count // STREAMS, None, weight_rows, feature_dev),
                    lambda k, s, i=i: (i, k, 0, 0),
                )
                for i in range(STREAMS)
            ]
            + [pl.BlockSpec(memory_space=pl.ANY)],
            out_specs=pl.BlockSpec((rows_dev, feature_dev), gathered_block),
        ),
        out_shape=struct((rows_dev, model), BF16),
        input_output_aliases={4 + STREAMS: 0},
        compiler_params=pltpu.CompilerParams(vmem_limit_bytes=VMEM_BYTES),
        cost_estimate=pl.CostEstimate(
            flops=2 * rows_dev * features * model,
            bytes_accessed=2 * features * model,
            transcendentals=0,
        ),
    )(place[1:], attended_rows, adapted, adapter_up_weight, *[gathered] * STREAMS, begun)
    return (mixed, down_gradient.T, up_gradient_sum)


def solution(mesh):
    in_specs = (P(), P(None, ("dp", "seq"), None), P(None, "seq"), P(), P(), P(("dp", "seq"), None))
    out_specs = (P(("dp", "seq"), None), P(), P())
    return jax.shard_map(body, mesh=mesh, in_specs=in_specs, out_specs=out_specs, check_vma=False)
```

```python
import functools
import math

import jax
import jax.numpy as jnp
import numpy as np
from jax import lax
from jax.experimental import pallas as pl
from jax.experimental.pallas import tpu as pltpu
from jax.sharding import PartitionSpec as P

HEAD = 128
SLOT = 64
ADAPTER_SCALE = 2.0
FAR = (3, 4, 5)
STREAMS = 4
VMEM_BYTES = 56 * 1024 * 1024
F32 = jnp.float32
BF16 = jnp.bfloat16


def contract(left, right, left_dim, right_dim):
    return lax.dot_general(
        left, right, (((left_dim,), (right_dim,)), ((), ())), preferred_element_type=F32
    )


def inverse_frequencies():
    sixth = HEAD // 6
    parts = []
    for width in (HEAD - 4 * sixth, 2 * sixth, 2 * sixth):
        exponent = np.arange(0, width, 2).astype(np.float32) / np.float32(width)
        parts.append(np.power(np.float32(10000.0), -exponent).astype(np.float32))
    return np.broadcast_to(np.repeat(np.concatenate(parts), 2)[None, :], (8, HEAD)).copy()


def iota(shape, dim):
    return lax.broadcasted_iota(jnp.int32, shape, dim)


def my_clips(table, group):
    def step(c, found):
        source, target = table[0, c], table[1, c]
        height, width = table[3, c], table[4, c]
        portion = table[2, c] * height * width // 8
        is_source, is_target = source == group, target == group
        chosen = (
            is_source & is_target,
            is_source & jnp.logical_not(is_target),
            is_target & jnp.logical_not(is_source),
        )
        mine = (c, portion, height, width)
        return tuple(
            tuple(jnp.where(hit, new, old) for new, old in zip(mine, clip))
            for hit, clip in zip(chosen, found)
        )

    zero = jnp.int32(0)
    blank = tuple((zero, zero, jnp.int32(1), jnp.int32(1)) for _ in range(3))
    return lax.fori_loop(0, table.shape[1], step, blank)


def placement(shape, row_dim, first, second):
    row = iota(shape, row_dim)
    slot_row = iota(shape, 1 - row_dim)
    in_second = slot_row >= SLOT
    token = jnp.where(in_second, slot_row - SLOT, slot_row)
    offset = jnp.where(in_second, second[0], first[0])
    portion = jnp.where(in_second, second[1], first[1])
    return jnp.where((row == token + offset) & (token < portion), 1.0, 0.0).astype(BF16)


def prepare(
    place, table, frequency, rows_far, cotangent_far, up, stay_out, move_out, to_rows, info,
    rows, cotangent, arrived,
):
    cotangent_copy = pltpu.make_async_copy(cotangent_far, cotangent, arrived.at[0])
    rows_copy = pltpu.make_async_copy(rows_far, rows, arrived.at[1])
    cotangent_copy.start()
    rows_copy.start()
    group, shard = place[0], place[1]
    stay, leave, arrive = my_clips(table, group)
    zero = jnp.int32(0)
    leave_offset = jnp.where(stay[0] < leave[0], stay[1], zero)
    stay_offset = jnp.where(leave[0] < stay[0], leave[1], zero)
    arrive_target = jnp.where(stay[0] < arrive[0], stay[1], zero)
    stay_target = jnp.where(arrive[0] < stay[0], arrive[1], zero)
    info[0] = stay[1]
    info[1] = arrive[1]
    count = rows.shape[1]
    select = placement(
        (2 * SLOT, count), 1, (stay_offset, stay[1]), (leave_offset, leave[1])
    )
    target_rows = placement(
        (cotangent.shape[0], 2 * SLOT), 0, (stay_target, stay[1]), (arrive_target, arrive[1])
    )
    to_rows[...] = target_rows

    shape = (2 * SLOT, HEAD)
    slot_row = iota(shape, 0)
    in_second = slot_row >= SLOT
    token = jnp.where(in_second, slot_row - SLOT, slot_row)
    portion = jnp.where(in_second, leave[1], stay[1])
    height = jnp.where(in_second, leave[2], stay[2]).astype(F32)
    width = jnp.where(in_second, leave[3], stay[3]).astype(F32)
    token = (token + shard * portion).astype(F32)
    row_of = jnp.floor((token + 0.5) / width)
    frame = jnp.floor((token + 0.5) / (height * width))
    sixth = HEAD // 6
    lane = iota(shape, 1)
    position = jnp.where(
        lane < HEAD - 4 * sixth,
        frame,
        jnp.where(lane < HEAD - 2 * sixth, row_of - frame * height, token - row_of * width),
    )
    angle = position * frequency[0:1, :]
    cosine, sine = jnp.cos(angle), jnp.sin(angle)
    even = lane % 2 == 0
    sine_next, sine_last = jnp.where(even, -sine, 0.0), jnp.where(even, 0.0, sine)

    cotangent_copy.wait()
    low = (ADAPTER_SCALE * contract(up[...], cotangent[...], 1, 1)).astype(BF16)
    low = contract(low, target_rows, 1, 0).astype(BF16)
    half = low.shape[0] // 2
    rows_copy.wait()

    width_dev = stay_out.shape[2]
    for k in range(8):
        column = k * width_dev
        for part in range(3):
            placed = contract(select, rows[part, :, pl.ds(column, width_dev)], 1, 0)
            if part < 2:
                turned = []
                for head in range(width_dev // HEAD):
                    lanes = slice(head * HEAD, (head + 1) * HEAD)
                    mine = placed[:, lanes]
                    turned.append(
                        mine * cosine
                        + pltpu.roll(mine, HEAD - 1, 1) * sine_next
                        + pltpu.roll(mine, 1, 1) * sine_last
                    )
                placed = jnp.concatenate(turned, axis=1)
            placed = placed.astype(BF16)
            stay_out[k, part * SLOT : (part + 1) * SLOT, :] = placed[:SLOT]
            start = (3 * k + part) * SLOT
            move_out[start : start + SLOT, :] = placed[SLOT:]
        stay_out[k, 3 * SLOT : 3 * SLOT + half, 0:HEAD] = low[:half]
        stay_out[k, 3 * SLOT : 3 * SLOT + half, HEAD : 2 * HEAD] = low[half:]
        stay_out[k, 3 * SLOT : 3 * SLOT + half, 2 * HEAD :] = jnp.zeros(
            (half, width_dev - 2 * HEAD), BF16
        )


def clip_attention(blocks, portion, store):
    width_dev = blocks[0].shape[1]
    total = 8 * SLOT
    scale = 1.0 / math.sqrt(HEAD)
    valid = lax.rem(iota((total, total), 1), SLOT) < portion
    for head in range(width_dev // HEAD):
        lanes = slice(head * HEAD, (head + 1) * HEAD)
        query, key, value = (
            jnp.concatenate(
                [blocks[k][part * SLOT : (part + 1) * SLOT, lanes] for k in range(8)], axis=0
            )
            for part in range(3)
        )
        scores = jnp.where(valid, contract(query, key, 1, 1) * scale, -1e30)
        largest = jnp.max(scores, axis=1, keepdims=True)
        weights = jnp.exp(scores - largest)
        weights = (weights / jnp.sum(weights, axis=1, keepdims=True)).astype(BF16)
        store(lanes, contract(weights, value, 1, 0).astype(BF16))


def attend_first(info, blocks, out):
    blocks = [blocks.at[k] for k in range(8)]

    def store(lanes, result):
        out[:, lanes] = result

    clip_attention(blocks, info[0], store)


def attend_second(info, first, extras, blocks, out, gradient, second):
    blocks = [blocks.at[k] for k in range(8)]

    def store(lanes, result):
        second[:, lanes] = result

    clip_attention(blocks, info[1], store)
    gradient_sum = jnp.zeros(gradient.shape, F32)
    half = gradient.shape[0] // 2
    for k in range(8):
        rows = slice(k * SLOT, (k + 1) * SLOT)
        out[k, :SLOT, :] = first[rows, :]
        out[k, SLOT:, :] = second[rows, :]
        extra = extras[k, 3 * SLOT : 3 * SLOT + half, :]
        low = jnp.concatenate([extra[:, 0:HEAD], extra[:, HEAD : 2 * HEAD]], axis=0)
        gradient_sum += contract(low, out[k], 1, 0)
    gradient[...] = gradient_sum


def up_gradient(back, to_rows, down, cotangent, down_part, attended, adapted_out, part_out, wide):
    width_dev = back.shape[2]
    for k in range(8):
        attended[:, k * width_dev : (k + 1) * width_dev] = contract(
            to_rows[...], back[k], 1, 0
        ).astype(BF16)
    adapted = contract(down[...], attended[...], 1, 1).astype(BF16)
    adapted_out[...] = adapted
    result = ADAPTER_SCALE * contract(adapted, cotangent[...], 1, 0)
    tiles = result.shape[1] // HEAD
    for j in range(tiles):
        wide[:, j, :] = result[:, j * HEAD : (j + 1) * HEAD]
    for j in range(down_part.shape[1] // HEAD):
        wide[:, tiles + j, :] = down_part[:, j * HEAD : (j + 1) * HEAD]
    for j in range(tiles + down_part.shape[1] // HEAD, wide.shape[1]):
        wide[:, j, :] = jnp.zeros((wide.shape[0], HEAD), F32)
    part_out[...] = wide[...].astype(BF16)


def add_and_repeat(parts, out):
    total = parts[0].astype(F32)
    for i in range(1, parts.shape[0]):
        total += parts[i].astype(F32)
    out[...] = jnp.broadcast_to(total[None], out.shape)


def join_and_repeat(tiles, parts, out, row):
    row[0:tiles, :] = jnp.sum(parts[:, 0:tiles, :], axis=0)
    each = (row.shape[0] - tiles) // 8
    for block in range(8):
        row[tiles + each * block : tiles + each * (block + 1), :] = parts[
            block, tiles : tiles + each, :
        ]
    out[...] = jnp.broadcast_to(row[...].astype(BF16)[None], out.shape)


def spread(parts, up_out, down_out, wide):
    wide[...] = parts[...].astype(F32)
    tiles = up_out.shape[1] // HEAD
    for j in range(tiles):
        up_out[:, j * HEAD : (j + 1) * HEAD] = wide[:, j, :]
    for j in range(down_out.shape[1] // HEAD):
        down_out[:, j * HEAD : (j + 1) * HEAD] = wide[:, tiles + j, :]


def project_own(shard, attended, adapted, up, own, out):
    extra = ADAPTER_SCALE * contract(adapted[...], up[...], 0, 0)
    out[...] = (contract(attended[...], own[...], 1, 0) + extra).astype(BF16)


def project(shard, attended, adapted, up, *refs):
    total = ADAPTER_SCALE * contract(adapted[...], up[...], 0, 0)
    depth = refs[0].shape[0] * refs[0].shape[1]
    for i in range(STREAMS):
        block = refs[i][...].reshape(depth, refs[i].shape[2])
        total += contract(attended[:, i * depth : (i + 1) * depth], block, 1, 0)
    refs[-1][...] = total.astype(BF16)


VM = pl.BlockSpec(memory_space=pltpu.VMEM)
SM = pl.BlockSpec(memory_space=pltpu.SMEM)
FAR_AWAY = pl.BlockSpec(memory_space=pl.ANY)


def call(kernel, in_specs, out_shapes, out_specs=None, flops=0, size=0, scratch=()):
    return pl.pallas_call(
        kernel,
        in_specs=in_specs,
        out_shape=out_shapes,
        out_specs=out_specs if out_specs is not None else jax.tree.map(lambda _: VM, out_shapes),
        scratch_shapes=scratch,
        compiler_params=pltpu.CompilerParams(vmem_limit_bytes=VMEM_BYTES),
        cost_estimate=pl.CostEstimate(flops=flops, bytes_accessed=size, transcendentals=0),
    )


def body(clip_table, attention_inputs, out_weight, adapter_down, adapter_up_weight, cotangent):
    dp_count, seq_count = lax.axis_size("dp"), lax.axis_size("seq")
    group, shard = lax.axis_index("dp"), lax.axis_index("seq")
    features = attention_inputs.shape[2]
    width_dev = features // seq_count
    feature_dev = out_weight.shape[1]
    rank, model = adapter_up_weight.shape
    rows_dev = cotangent.shape[0]
    place = jnp.stack([group, shard]).astype(jnp.int32)
    struct = jax.ShapeDtypeStruct

    def turn(block, k):
        return lax.ppermute(block, "seq", [(i, (i + k) % seq_count) for i in range(seq_count)])

    weight_rows = features // dp_count
    own_rows = lax.dynamic_slice_in_dim(out_weight, group * weight_rows, weight_rows, 0)
    near = {k: turn(own_rows, -k) for k in range(1, seq_count) if k not in FAR}

    prepared = call(
        prepare,
        [SM, SM, VM, FAR_AWAY, FAR_AWAY, VM],
        [
            struct((seq_count, 3 * SLOT + rank // 2, width_dev), BF16),
            struct((seq_count * 3 * SLOT, width_dev), BF16),
            struct((rows_dev, 2 * SLOT), BF16),
            struct((2,), jnp.int32),
        ],
        [VM] * 3 + [SM],
        scratch=[
            pltpu.VMEM(attention_inputs.shape, BF16),
            pltpu.VMEM(cotangent.shape, BF16),
            pltpu.SemaphoreType.DMA((2,)),
        ],
        flops=10**9,
        size=6 * 10**6,
    )(
        place,
        clip_table.T,
        jnp.asarray(inverse_frequencies()),
        attention_inputs,
        cotangent,
        adapter_up_weight,
    )
    stay, moving, to_rows, info = prepared

    def exchange(block, axis):
        return lax.all_to_all(block, axis, split_axis=0, concat_axis=0, tiled=True)

    apart = jnp.bitwise_xor(clip_table[:, 0], clip_table[:, 1])
    bits = dp_count.bit_length() - 1
    branch = jnp.max(sum((apart > (1 << b)).astype(jnp.int32) for b in range(bits - 1)))

    def move(bit, moving, stay, pair, below):
        moved = lax.ppermute(moving, "dp", [(g, g ^ (1 << bit)) for g in range(dp_count)])
        return moved, exchange(stay, "seq"), turn(pair, -2), turn(below, 1)

    pair = jnp.concatenate([near[1], near[2]], axis=0)
    moving, pair, *blocks = lax.optimization_barrier((moving, pair, *near.values()))
    blocks = dict(zip(near, blocks))
    moved, stay, *far = lax.switch(
        branch,
        [functools.partial(move, bit) for bit in range(bits)],
        moving,
        stay,
        pair,
        blocks[6],
    )
    others = jnp.concatenate([pair, blocks[6], blocks[7], *far], axis=0)
    others, moved, stay = lax.optimization_barrier((others, moved, stay))
    gathered = lax.all_gather(others, "dp", axis=0, tiled=True)
    gathered = gathered.reshape(dp_count, seq_count - 1, weight_rows, feature_dev)
    moved = exchange(moved.reshape(seq_count, 3 * SLOT, width_dev), "seq")
    first = call(
        attend_first,
        [SM, VM],
        struct((seq_count * SLOT, width_dev), BF16),
        VM,
        flops=10**9,
        size=2 * 10**6,
    )(info, stay)
    attended, down_part = call(
        attend_second,
        [SM] + [VM] * 3,
        [struct((seq_count, 2 * SLOT, width_dev), BF16), struct((rank, width_dev), F32)],
        flops=10**9,
        size=4 * 10**6,
        scratch=[pltpu.VMEM((seq_count * SLOT, width_dev), BF16)],
    )(info, first, stay, moved)
    back = exchange(attended, "seq")

    up_tiles, down_tiles = model // HEAD, features // HEAD
    piece_tiles = -(-(up_tiles + down_tiles // seq_count) // 16) * 16
    attended_rows, adapted, mine = call(
        up_gradient,
        [VM] * 5,
        [
            struct((rows_dev, features), BF16),
            struct((rank, rows_dev), BF16),
            struct((rank, piece_tiles, HEAD), BF16),
        ],
        flops=10**8,
        size=2 * 10**6,
        scratch=[pltpu.VMEM((rank, piece_tiles, HEAD), F32)],
    )(back, to_rows, adapter_down.T, cotangent, down_part)
    mine = exchange(mine, "dp")
    mine = call(add_and_repeat, [VM], struct((seq_count, piece_tiles, HEAD), F32), VM)(mine)

    def whole(shape):
        return pl.BlockSpec(shape, lambda k, s: (0,) * len(shape))

    def own_block(k, s):
        return (0, s[0])

    def gathered_block(k, s):
        away = jnp.where(k < 2, k + 1, jnp.where(k < 4, k + 4, k - 1))
        return (0, lax.rem(s[0] + away, 8))

    begun = pl.pallas_call(
        project_own,
        grid_spec=pltpu.PrefetchScalarGridSpec(
            num_scalar_prefetch=1,
            grid=(1,),
            in_specs=[
                whole((rows_dev, features)),
                whole((rank, rows_dev)),
                pl.BlockSpec((rank, feature_dev), own_block),
                whole((features, feature_dev)),
            ],
            out_specs=pl.BlockSpec((rows_dev, feature_dev), own_block),
        ),
        out_shape=struct((rows_dev, model), BF16),
        compiler_params=pltpu.CompilerParams(vmem_limit_bytes=VMEM_BYTES),
        cost_estimate=pl.CostEstimate(
            flops=2 * rows_dev * features * feature_dev,
            bytes_accessed=2 * features * feature_dev,
            transcendentals=0,
        ),
    )(place[1:], attended_rows, adapted, adapter_up_weight, out_weight)

    mine = exchange(mine, "seq")
    mine = call(
        functools.partial(join_and_repeat, up_tiles),
        [VM],
        struct((dp_count, up_tiles + down_tiles, HEAD), BF16),
        VM,
        scratch=[pltpu.VMEM((up_tiles + down_tiles, HEAD), F32)],
    )(mine)
    mine, begun, gathered = lax.optimization_barrier((mine, begun, gathered))
    mine = exchange(mine, "dp")
    up_gradient_sum, down_gradient = call(
        spread,
        [VM],
        [struct((rank, model), F32), struct((rank, features), F32)],
        scratch=[pltpu.VMEM((dp_count, up_tiles + down_tiles, HEAD), F32)],
    )(mine)

    mixed = pl.pallas_call(
        project,
        grid_spec=pltpu.PrefetchScalarGridSpec(
            num_scalar_prefetch=1,
            grid=(seq_count - 1,),
            in_specs=[
                whole((rows_dev, features)),
                whole((rank, rows_dev)),
                pl.BlockSpec((rank, feature_dev), gathered_block),
            ]
            + [
                pl.BlockSpec(
                    (dp_count // STREAMS, None, weight_rows, feature_dev),
                    lambda k, s, i=i: (i, k, 0, 0),
                )
                for i in range(STREAMS)
            ]
            + [pl.BlockSpec(memory_space=pl.ANY)],
            out_specs=pl.BlockSpec((rows_dev, feature_dev), gathered_block),
        ),
        out_shape=struct((rows_dev, model), BF16),
        input_output_aliases={4 + STREAMS: 0},
        compiler_params=pltpu.CompilerParams(vmem_limit_bytes=VMEM_BYTES),
        cost_estimate=pl.CostEstimate(
            flops=2 * rows_dev * features * model,
            bytes_accessed=2 * features * model,
            transcendentals=0,
        ),
    )(place[1:], attended_rows, adapted, adapter_up_weight, *[gathered] * STREAMS, begun)
    return (mixed, down_gradient.T, up_gradient_sum)


def solution(mesh):
    in_specs = (P(), P(None, ("dp", "seq"), None), P(None, "seq"), P(), P(), P(("dp", "seq"), None))
    out_specs = (P(("dp", "seq"), None), P(), P())
    return jax.shard_map(body, mesh=mesh, in_specs=in_specs, out_specs=out_specs, check_vma=False)
```
